32 devices in a mesh: grp: 2 (over x), gx: 16 (over z, y, core).
Axes of the slice: x: 2, y: 2, z: 4, core: 2. Of those that a mesh axis runs over, the one named last changes fastest.
Arguments:
- field: float32 [32, 1024, 1024], P('grp', 'gx'), parts along dimension 0, may hold values from -150 to 150
- basis_one: float32 [2048, 256], P('grp'), parts along dimension 0, may hold values from -0.1875 to 0.1875
- start: float32 [1024, 256], replicated, may hold values from -6 to 6
Outputs:
- basis_two: float32 [2048, 256], P('grp'), parts along dimension 0
- core: float32 [32, 256, 256], P(('grp', 'gx')), parts along dimension 0
The draws below stay inside these ranges and needn't reach their ends.
There are 2 independent parts, one for each index of `grp`. The reference program is written for one: setup_inputs(seed, part) draws one part's arguments, and reference() takes and returns one part's arrays. A program takes and returns all parts, laid end to end along the dimension named above; an argument that names none is the same for every part. Nothing has to cross between parts.
All inputs are finite; a program needn't handle non-finite values.
Results may differ from the reference program's by a relative error of at most 0.0003.
Values sent between devices are 32-bit elements; how exact they have to be, the bound alone decides.
A program may use at most 128 MiB of HBM per device.

```python
import math
import jax
import jax.numpy as jnp
from jax import lax

I1 = 1024
I2 = 1024
R1 = 256
R2 = 256
ITERS = 4
I3 = 16


def draw_field(key, part):
    key = jax.random.fold_in(key, 11)
    keys = jax.random.split(key, 5)
    noise = jnp.clip(jax.random.normal(keys[0], (I3, I1, I2), jnp.float32), -6.0, 6.0)
    weight = 0.5
    ramp = jnp.arange(I3, dtype=jnp.float32).reshape(I3, 1, 1) / I3
    plane = jnp.exp(math.log(3.0) * ramp + jax.random.uniform(keys[1], (I3, 1, 1), jnp.float32, 0.0, math.log(3.0)))
    column = jnp.exp(jax.random.uniform(keys[2], (1, 1, I2), jnp.float32, -math.log(2.0), math.log(2.0)))
    amounts = jax.random.uniform(keys[3], (I3, I1, 4), jnp.float32, -1.0, 1.0)
    directs = jax.random.uniform(keys[4], (4, I2), jnp.float32, -1.0, 1.0)
    common = jnp.zeros((I3, I1, I2), jnp.float32)
    for index in range(4):
        common = common + amounts[:, :, index:index + 1] * directs[index].reshape(1, 1, I2)
    return (noise * column + weight * common) * plane


def scatter_about(rng, extent, spread, most, kind=jnp.bfloat16):
    return jnp.clip(spread * jax.random.normal(rng, extent, jnp.float32), -most, most).astype(kind)


def setup_inputs(seed: int = 0, part: int = 0) -> dict:
    arg_keys = jax.random.split(jax.random.key(seed), 4)
    part_keys = jax.random.split(jax.random.fold_in(arg_keys[3], part), 4)
    field = draw_field(jax.random.fold_in(jax.random.fold_in(arg_keys[3], part), 71), part)
    basis_one = scatter_about(part_keys[1], (I1, R1), I1 ** -0.5, 0.1875, jnp.float32)
    start = scatter_about(arg_keys[2], (I2, R2), 1.0, 6.0, jnp.float32)
    return {"field": field, "basis_one": basis_one, "start": start}


def reference(field, basis_one, start):
    highest = lax.Precision.HIGHEST
    compressed = jnp.einsum('ir,kij->krj', basis_one, field, precision=highest)
    gram = jnp.einsum('kri,krj->ij', compressed, compressed, precision=highest)
    iterate = start
    for step in range(ITERS):
        product = jnp.dot(gram, iterate, precision=highest)
        cross = jnp.dot(product.T, product, precision=highest)
        factor = jnp.linalg.cholesky(cross)
        iterate = jax.scipy.linalg.solve_triangular(factor, product.T, lower=True).T
    core = jnp.einsum('krj,js->krs', compressed, iterate, precision=highest)
    return (iterate, core)
```

```python
import jax
import jax.numpy as jnp
from jax import lax
from jax.sharding import PartitionSpec as P

ITERS = 4
BLOCK = 128
HIGHEST = lax.Precision.HIGHEST


def packed_gram(compressed):
    width = compressed.shape[2]
    rows = [
        jnp.einsum("kri,krj->ij", compressed[:, :, at:at + BLOCK], compressed[:, :, at:], precision=HIGHEST)
        for at in range(0, width, BLOCK)
    ]
    return jnp.concatenate(rows, axis=1)


def unpacked_gram(packed, width):
    rows, offset = [], 0
    for at in range(0, width, BLOCK):
        rows.append(packed[:, offset:offset + width - at])
        offset += width - at
    whole = []
    for a in range(len(rows)):
        below = [rows[b][:, (a - b) * BLOCK:(a - b + 1) * BLOCK].T for b in range(a)]
        whole.append(jnp.concatenate(below + [rows[a]], axis=1))
    return jnp.concatenate(whole, axis=0)


def body(field, basis_one, start):
    planes = lax.all_to_all(field, "gx", split_axis=0, concat_axis=1, tiled=True)
    compressed = jnp.einsum("ir,kij->krj", basis_one, planes, precision=HIGHEST)
    gram = unpacked_gram(lax.psum(packed_gram(compressed), "gx"), compressed.shape[2])
    iterate = start
    for step in range(ITERS):
        product = jnp.dot(gram, iterate, precision=HIGHEST)
        cross = jnp.dot(product.T, product, precision=HIGHEST)
        factor = jnp.linalg.cholesky(cross)
        iterate = jax.scipy.linalg.solve_triangular(factor, product.T, lower=True).T
    core = jnp.einsum("krj,js->krs", compressed, iterate, precision=HIGHEST)
    return (iterate, core)


def solution(mesh):
    in_specs = (P("grp", "gx", None), P("grp", None), P())
    out_specs = (P("grp", None), P(("grp", "gx"), None, None))
    return jax.shard_map(body, mesh=mesh, in_specs=in_specs, out_specs=out_specs, check_vma=False)
```

```python
import jax
import jax.numpy as jnp
from jax import lax
from jax.experimental import pallas as pl
from jax.experimental.pallas import tpu as pltpu
from jax.sharding import PartitionSpec as P

ITERS = 4
BLOCK = 128
SUB = 8
HIGHEST = lax.Precision.HIGHEST


def packed_gram(compressed):
    width = compressed.shape[2]
    rows = [
        jnp.einsum("kri,krj->ij", compressed[:, :, at:at + BLOCK], compressed[:, :, at:], precision=HIGHEST)
        for at in range(0, width, BLOCK)
    ]
    return jnp.concatenate(rows, axis=1)


def unpacked_gram(packed, width):
    rows, offset = [], 0
    for at in range(0, width, BLOCK):
        rows.append(packed[:, offset:offset + width - at])
        offset += width - at
    whole = []
    for a in range(len(rows)):
        below = [rows[b][:, (a - b) * BLOCK:(a - b + 1) * BLOCK].T for b in range(a)]
        whole.append(jnp.concatenate(below + [rows[a]], axis=1))
    return jnp.concatenate(whole, axis=0)


def block_inverse(block):
    size = block.shape[0]
    sub = lax.broadcasted_iota(jnp.int32, (SUB, size), 0)
    lane = lax.broadcasted_iota(jnp.int32, (SUB, size), 1)
    tiles = size // SUB
    left = [block[t * SUB:(t + 1) * SUB, :] for t in range(tiles)]
    right = [jnp.where(lane == sub + t * SUB, 1.0, 0.0).astype(jnp.float32) for t in range(tiles)]
    done = [jnp.zeros((SUB, size), jnp.float32) for t in range(tiles)]

    def row(tile, at):
        return jnp.broadcast_to(tile[at:at + 1, :], (SUB, size))

    def column(tile, at):
        return jnp.broadcast_to(tile[:, at:at + 1], (SUB, size))

    for j in range(0, size, 4):
        tile, at = j // SUB, j % SUB
        m = [row(left[tile], at + k) for k in range(4)]
        n = [row(right[tile], at + k) for k in range(4)]
        cols = [column(left[tile], j + l) for l in range(4)]
        d = [[row(cols[l], at + k) for l in range(k + 1)] for k in range(4)]
        qa = 1.0 / (d[0][0] * d[1][1] - d[1][0] * d[1][0])
        g = {}
        for i in (2, 3):
            g[i, 0] = (d[1][1] * d[i][0] - d[1][0] * d[i][1]) * qa
            g[i, 1] = (d[0][0] * d[i][1] - d[1][0] * d[i][0]) * qa
        e22 = d[2][2] - (g[2, 0] * d[2][0] + g[2, 1] * d[2][1])
        e32 = d[3][2] - (g[3, 0] * d[2][0] + g[3, 1] * d[2][1])
        e33 = d[3][3] - (g[3, 0] * d[3][0] + g[3, 1] * d[3][1])
        qb = 1.0 / (e22 * e33 - e32 * e32)

        def weights(v):
            a0 = (d[1][1] * v[0] - d[1][0] * v[1]) * qa
            a1 = (d[0][0] * v[1] - d[1][0] * v[0]) * qa
            v2 = v[2] - (g[2, 0] * v[0] + g[2, 1] * v[1])
            v3 = v[3] - (g[3, 0] * v[0] + g[3, 1] * v[1])
            b0 = (e33 * v2 - e32 * v3) * qb
            b1 = (e22 * v3 - e32 * v2) * qb
            return (a0 - g[2, 0] * b0 - g[3, 0] * b1, a1 - g[2, 1] * b0 - g[3, 1] * b1, b0, b1), v2, v3

        wm, _, _ = weights(m)
        wn, n2, n3 = weights(n)
        ra = 1.0 / d[0][0]
        rb = 1.0 / e22
        n1 = n[1] - d[1][0] * ra * n[0]
        n3 = n3 - e32 * rb * n2
        p1 = d[1][1] - d[1][0] * d[1][0] * ra
        p3 = e33 - e32 * e32 * rb
        rows = (n[0] * lax.rsqrt(d[0][0]), n1 * lax.rsqrt(p1), n2 * lax.rsqrt(e22), n3 * lax.rsqrt(p3))
        for k in range(4):
            done[tile] = jnp.where(sub == at + k, rows[k], done[tile])
        for t in range(tile, tiles):
            if t == tile and at != 0:
                continue
            c = cols if t == tile else [column(left[t], j + l) for l in range(4)]
            if t == tile:
                c = [jnp.where(sub >= at + 4, v, 0.0) for v in c]
            left[t] = left[t] - ((c[0] * wm[0] + c[1] * wm[1]) + (c[2] * wm[2] + c[3] * wm[3]))
            right[t] = right[t] - ((c[0] * wn[0] + c[1] * wn[1]) + (c[2] * wn[2] + c[3] * wn[3]))
    return jnp.concatenate(done, axis=0)


def dot_t(a, b):
    return lax.dot_general(a, b, (((1,), (1,)), ((), ())), precision=HIGHEST, preferred_element_type=jnp.float32)


def dot(a, b):
    return jnp.dot(a, b, precision=HIGHEST, preferred_element_type=jnp.float32)


def factor_kernel(cross_ref, inverse_ref, work_ref, part_ref):
    size = cross_ref.shape[0]
    half = size // 2
    cross = cross_ref[...]
    eye = lax.broadcasted_iota(jnp.int32, (size, size), 0) == lax.broadcasted_iota(jnp.int32, (size, size), 1)
    diagonal = jnp.where(eye, cross, 0.0)
    along = lax.rsqrt(jnp.sum(diagonal, axis=0, keepdims=True))
    down = lax.rsqrt(jnp.sum(diagonal, axis=1, keepdims=True))
    work_ref[...] = cross * down * along
    part_ref[0] = work_ref[:half, :half]

    def step(index, carry):
        part_ref[index] = block_inverse(part_ref[index])

        @pl.when(index == 0)
        def _():
            side = dot_t(work_ref[half:, :half], part_ref[0])
            work_ref[half:, :half] = side
            part_ref[1] = work_ref[half:, half:] - dot_t(side, side)

        return carry

    lax.fori_loop(0, 2, step, 0)
    first, second = part_ref[0], part_ref[1]
    corner = -dot(dot(second, work_ref[half:, :half]), first)
    inverse_ref[:half, :half] = first * along[:, :half]
    inverse_ref[:half, half:] = jnp.zeros((half, half), jnp.float32)
    inverse_ref[half:, :half] = corner * along[:, :half]
    inverse_ref[half:, half:] = second * along[:, half:]


def factor_inverse(cross):
    size = cross.shape[0]
    return pl.pallas_call(
        factor_kernel,
        out_shape=jax.ShapeDtypeStruct((size, size), jnp.float32),
        in_specs=[pl.BlockSpec(memory_space=pltpu.VMEM)],
        out_specs=pl.BlockSpec(memory_space=pltpu.VMEM),
        scratch_shapes=[pltpu.VMEM((size, size), jnp.float32), pltpu.VMEM((2, size // 2, size // 2), jnp.float32)],
        compiler_params=pltpu.CompilerParams(vmem_limit_bytes=32 * 2**20),
        name="factor_inverse",
    )(cross)


def body(field, basis_one, start):
    planes = lax.all_to_all(field, "gx", split_axis=0, concat_axis=1, tiled=True)
    compressed = jnp.einsum("ir,kij->krj", basis_one, planes, precision=HIGHEST)
    gram = unpacked_gram(lax.psum(packed_gram(compressed), "gx"), compressed.shape[2])
    iterate = start
    for step in range(ITERS):
        product = jnp.dot(gram, iterate, precision=HIGHEST)
        cross = jnp.dot(product.T, product, precision=HIGHEST)
        iterate = jnp.einsum("js,rs->jr", product, factor_inverse(cross), precision=HIGHEST)
    core = jnp.einsum("krj,js->krs", compressed, iterate, precision=HIGHEST)
    return (iterate, core)


def solution(mesh):
    in_specs = (P("grp", "gx", None), P("grp", None), P())
    out_specs = (P("grp", None), P(("grp", "gx"), None, None))
    return jax.shard_map(body, mesh=mesh, in_specs=in_specs, out_specs=out_specs, check_vma=False)
```

```python
import jax
import jax.numpy as jnp
from jax import lax
from jax.experimental import pallas as pl
from jax.experimental.pallas import tpu as pltpu
from jax.sharding import PartitionSpec as P

ITERS = 4
BLOCK = 128
SUB = 8
HIGHEST = lax.Precision.HIGHEST


def packed_gram(compressed):
    width = compressed.shape[2]
    rows = [
        jnp.einsum("kri,krj->ij", compressed[:, :, at:at + BLOCK], compressed[:, :, at:], precision=HIGHEST)
        for at in range(0, width, BLOCK)
    ]
    return jnp.concatenate(rows, axis=1)


def unpacked_gram(packed, width):
    rows, offset = [], 0
    for at in range(0, width, BLOCK):
        rows.append(packed[:, offset:offset + width - at])
        offset += width - at
    whole = []
    for a in range(len(rows)):
        below = [rows[b][:, (a - b) * BLOCK:(a - b + 1) * BLOCK].T for b in range(a)]
        whole.append(jnp.concatenate(below + [rows[a]], axis=1))
    return jnp.concatenate(whole, axis=0)


def block_inverse(block):
    size = block.shape[0]
    sub = lax.broadcasted_iota(jnp.int32, (SUB, size), 0)
    lane = lax.broadcasted_iota(jnp.int32, (SUB, size), 1)
    tiles = size // SUB
    left = [block[t * SUB:(t + 1) * SUB, :] for t in range(tiles)]
    right = [jnp.where(lane == sub + t * SUB, 1.0, 0.0).astype(jnp.float32) for t in range(tiles)]
    done = [jnp.zeros((SUB, size), jnp.float32) for t in range(tiles)]

    def row(tile, at):
        return jnp.broadcast_to(tile[at:at + 1, :], (SUB, size))

    def column(tile, at):
        return jnp.broadcast_to(tile[:, at:at + 1], (SUB, size))

    for j in range(0, size, 4):
        tile, at = j // SUB, j % SUB
        m = [row(left[tile], at + k) for k in range(4)]
        n = [row(right[tile], at + k) for k in range(4)]
        cols = [column(left[tile], j + l) for l in range(4)]
        d = [[row(cols[l], at + k) for l in range(k + 1)] for k in range(4)]
        qa = 1.0 / (d[0][0] * d[1][1] - d[1][0] * d[1][0])
        g = {}
        for i in (2, 3):
            g[i, 0] = (d[1][1] * d[i][0] - d[1][0] * d[i][1]) * qa
            g[i, 1] = (d[0][0] * d[i][1] - d[1][0] * d[i][0]) * qa
        e22 = d[2][2] - (g[2, 0] * d[2][0] + g[2, 1] * d[2][1])
        e32 = d[3][2] - (g[3, 0] * d[2][0] + g[3, 1] * d[2][1])
        e33 = d[3][3] - (g[3, 0] * d[3][0] + g[3, 1] * d[3][1])
        qb = 1.0 / (e22 * e33 - e32 * e32)

        def weights(v):
            a0 = (d[1][1] * v[0] - d[1][0] * v[1]) * qa
            a1 = (d[0][0] * v[1] - d[1][0] * v[0]) * qa
            v2 = v[2] - (g[2, 0] * v[0] + g[2, 1] * v[1])
            v3 = v[3] - (g[3, 0] * v[0] + g[3, 1] * v[1])
            b0 = (e33 * v2 - e32 * v3) * qb
            b1 = (e22 * v3 - e32 * v2) * qb
            return (a0 - g[2, 0] * b0 - g[3, 0] * b1, a1 - g[2, 1] * b0 - g[3, 1] * b1, b0, b1), v2, v3

        wm, _, _ = weights(m)
        wn, n2, n3 = weights(n)
        ra = 1.0 / d[0][0]
        rb = 1.0 / e22
        n1 = n[1] - d[1][0] * ra * n[0]
        n3 = n3 - e32 * rb * n2
        p1 = d[1][1] - d[1][0] * d[1][0] * ra
        p3 = e33 - e32 * e32 * rb
        rows = (n[0] * lax.rsqrt(d[0][0]), n1 * lax.rsqrt(p1), n2 * lax.rsqrt(e22), n3 * lax.rsqrt(p3))
        for k in range(4):
            done[tile] = jnp.where(sub == at + k, rows[k], done[tile])
        for t in range(tile, tiles):
            if t == tile and at != 0:
                continue
            c = cols if t == tile else [column(left[t], j + l) for l in range(4)]
            if t == tile:
                c = [jnp.where(sub >= at + 4, v, 0.0) for v in c]
            left[t] = left[t] - ((c[0] * wm[0] + c[1] * wm[1]) + (c[2] * wm[2] + c[3] * wm[3]))
            right[t] = right[t] - ((c[0] * wn[0] + c[1] * wn[1]) + (c[2] * wn[2] + c[3] * wn[3]))
    return jnp.concatenate(done, axis=0)


def dot_t(a, b):
    return lax.dot_general(a, b, (((1,), (1,)), ((), ())), precision=HIGHEST, preferred_element_type=jnp.float32)


def dot(a, b):
    return jnp.dot(a, b, precision=HIGHEST, preferred_element_type=jnp.float32)


def halves_of(value):
    high = value.astype(jnp.bfloat16)
    return high, (value - high.astype(jnp.float32)).astype(jnp.bfloat16)


def dot_halves(a, b):
    def one(x, y):
        return jnp.dot(x, y, preferred_element_type=jnp.float32)

    return one(a[0], b[0]) + (one(a[1], b[0]) + one(a[0], b[1]))


def factor_inverse(cross, inverse_ref, work_ref, part_ref):
    size = cross.shape[0]
    half = size // 2
    eye = lax.broadcasted_iota(jnp.int32, (size, size), 0) == lax.broadcasted_iota(jnp.int32, (size, size), 1)
    diagonal = jnp.where(eye, cross, 0.0)
    along = lax.rsqrt(jnp.sum(diagonal, axis=0, keepdims=True))
    down = lax.rsqrt(jnp.sum(diagonal, axis=1, keepdims=True))
    work_ref[...] = cross * down * along
    part_ref[0] = work_ref[:half, :half]

    def step(index, carry):
        part_ref[index] = block_inverse(part_ref[index])

        @pl.when(index == 0)
        def _():
            side = dot_t(work_ref[half:, :half], part_ref[0])
            work_ref[half:, :half] = side
            part_ref[1] = work_ref[half:, half:] - dot_t(side, side)

        return carry

    lax.fori_loop(0, 2, step, 0)
    first, second = part_ref[0], part_ref[1]
    corner = -dot(dot(second, work_ref[half:, :half]), first)
    inverse_ref[:half, :half] = first * along[:, :half]
    inverse_ref[:half, half:] = jnp.zeros((half, half), jnp.float32)
    inverse_ref[half:, :half] = corner * along[:, :half]
    inverse_ref[half:, half:] = second * along[:, half:]


def subspace_kernel(gram_ref, start_ref, basis_ref, turned_ref, high_ref, low_ref, product_ref, inverse_ref, work_ref,
                    part_ref):
    high_ref[...], low_ref[...] = halves_of(gram_ref[...])
    turned_ref[...] = start_ref[...].T

    def step(index, carry):
        product_ref[...] = dot_halves(halves_of(turned_ref[...]), (high_ref[...], low_ref[...]))
        product = product_ref[...]
        factor_inverse(dot_t(product, product), inverse_ref, work_ref, part_ref)
        turned_ref[...] = dot_halves(halves_of(inverse_ref[...]), halves_of(product_ref[...]))
        return carry

    lax.fori_loop(0, ITERS, step, 0)
    basis_ref[...] = turned_ref[...].T


def subspace(gram, start):
    width, rank = start.shape
    vmem = pl.BlockSpec(memory_space=pltpu.VMEM)
    return pl.pallas_call(
        subspace_kernel,
        out_shape=(jax.ShapeDtypeStruct((width, rank), jnp.float32), jax.ShapeDtypeStruct((rank, width), jnp.float32)),
        in_specs=[vmem, vmem],
        out_specs=(vmem, vmem),
        scratch_shapes=[
            pltpu.VMEM((width, width), jnp.bfloat16),
            pltpu.VMEM((width, width), jnp.bfloat16),
            pltpu.VMEM((rank, width), jnp.float32),
            pltpu.VMEM((rank, rank), jnp.float32),
            pltpu.VMEM((rank, rank), jnp.float32),
            pltpu.VMEM((2, rank // 2, rank // 2), jnp.float32),
        ],
        compiler_params=pltpu.CompilerParams(vmem_limit_bytes=40 * 2**20),
        name="subspace",
    )(gram, start)


HALVES = ((0, 1, 5), (2, 3, 4, 6, 7))


def use_kernel(ranks, width):
    return ranks == 16 and width == 8 * BLOCK


def sum_kernel(part_ref, gram_ref, total, side, near, far, near_sum, far_sum, send_sems, recv_sems):
    me = lax.axis_index("gx")
    c, b, a = lax.rem(me, 2), lax.rem(me // 2, 2), me // 4
    sibling = me + 1 - 2 * c
    across = me + 2 - 4 * b
    others = [lax.rem(a + d, 4) * 4 + b * 2 + c for d in (1, 2, 3)]
    places = [lax.rem(a + d, 4) for d in (1, 2, 3)]

    barrier = pltpu.get_barrier_semaphore()
    for device in [sibling, across] + others:
        pl.semaphore_signal(barrier, inc=1, device_id={"gx": device}, device_id_type=pl.DeviceIdType.MESH)
    pl.semaphore_wait(barrier, 5)

    def send(slot, source, target, device):
        copy = pltpu.make_async_remote_copy(
            src_ref=source, dst_ref=target, send_sem=send_sems.at[slot], recv_sem=recv_sems.at[slot],
            device_id={"gx": device}, device_id_type=pl.DeviceIdType.MESH)
        copy.start()
        return copy

    def rows(start, count):
        return pl.ds(pl.multiple_of(start, SUB), count)

    def finish(copies):
        for copy in copies:
            copy.wait()

    scatter = [send(h, part_ref.at[h, rows((1 - c) * 64, 64)], side.at[h], sibling) for h in (0, 1)]
    scatter[0].wait()
    side[0] = side[0] + part_ref[0, rows(c * 64, 64), :]
    first_near = send(2, side.at[0, rows((1 - b) * 32, 32)], near.at[0, pl.ds(0, 32)], across)
    scatter[1].wait()
    side[1] = side[1] + part_ref[1, rows(c * 64, 64), :]
    first_far = [
        send(3 + d, side.at[1, rows(places[d] * 16, 16)], far.at[1, d, pl.ds(0, 16)], others[d]) for d in range(3)
    ]
    first_near.wait()
    near_sum[...] = side[0, rows(b * 32, 32), :] + near[0]
    second_far = [
        send(6 + d, near_sum.at[rows(places[d] * 8, 8)], far.at[0, d, pl.ds(0, 8)], others[d]) for d in range(3)
    ]
    finish(first_far)
    far_sum[...] = side[1, rows(a * 16, 16), :] + (far[1, 0] + far[1, 1] + far[1, 2])
    second_near = send(9, far_sum.at[rows((1 - b) * 8, 8)], near.at[1, pl.ds(0, 8)], across)
    finish(second_far)
    own_first = c * 64 + b * 32 + a * 8
    total[0, rows(own_first, 8), :] = near_sum[rows(a * 8, 8), :] + (
        far[0, 0, :8, :] + far[0, 1, :8, :] + far[0, 2, :8, :])
    piece = total.at[0, rows(own_first, 8)]
    gather_far = [send(10 + d, piece, piece, others[d]) for d in range(3)]
    second_near.wait()
    own_second = c * 64 + a * 16 + b * 8
    total[1, rows(own_second, 8), :] = far_sum[rows(b * 8, 8), :] + near[1, :8, :]
    piece = total.at[1, rows(own_second, 8)]
    gather_near = send(13, piece, piece, across)
    finish(gather_far)
    piece = total.at[0, rows(c * 64 + b * 32, 32)]
    last_near = send(14, piece, piece, across)
    gather_near.wait()
    piece = total.at[1, rows(c * 64 + a * 16, 16)]
    last_far = [send(15 + d, piece, piece, others[d]) for d in range(3)]
    last_near.wait()
    piece = total.at[0, rows(c * 64, 64)]
    gather = [send(18, piece, piece, sibling)]
    finish(last_far)
    piece = total.at[1, rows(c * 64, 64)]
    gather.append(send(19, piece, piece, sibling))
    for h in (0, 1):
        gather[h].wait()
        offset = 0
        for r in HALVES[h]:
            for s in range(r, 8):
                tile = total[h, :, offset * BLOCK:(offset + 1) * BLOCK]
                gram_ref[r * BLOCK:(r + 1) * BLOCK, s * BLOCK:(s + 1) * BLOCK] = tile
                if s != r:
                    gram_ref[s * BLOCK:(s + 1) * BLOCK, r * BLOCK:(r + 1) * BLOCK] = tile.T
                offset += 1


def summed_gram(compressed):
    width = compressed.shape[2]
    terms = [
        jnp.concatenate(
            [jnp.einsum("kri,krj->ij", compressed[:, :, r * BLOCK:(r + 1) * BLOCK], compressed[:, :, r * BLOCK:],
                        precision=lax.Precision.HIGH) for r in half], axis=1)
        for half in HALVES
    ]
    part = jnp.stack(terms)
    columns = part.shape[2]
    vmem = pl.BlockSpec(memory_space=pltpu.VMEM)
    return pl.pallas_call(
        sum_kernel,
        out_shape=jax.ShapeDtypeStruct((width, width), jnp.float32),
        in_specs=[vmem],
        out_specs=vmem,
        scratch_shapes=[
            pltpu.VMEM((2, BLOCK, columns), jnp.float32),
            pltpu.VMEM((2, 64, columns), jnp.float32),
            pltpu.VMEM((2, 32, columns), jnp.float32),
            pltpu.VMEM((2, 3, 16, columns), jnp.float32),
            pltpu.VMEM((32, columns), jnp.float32),
            pltpu.VMEM((16, columns), jnp.float32),
            pltpu.SemaphoreType.DMA((20,)),
            pltpu.SemaphoreType.DMA((20,)),
        ],
        compiler_params=pltpu.CompilerParams(collective_id=0, has_side_effects=True, vmem_limit_bytes=40 * 2**20),
        name="sum_gram",
    )(part)


def body(field, basis_one, start):
    planes = lax.all_to_all(field, "gx", split_axis=0, concat_axis=1, tiled=True)
    compressed = jnp.einsum("ir,kij->krj", basis_one, planes, precision=lax.Precision.HIGH)
    if use_kernel(lax.axis_size("gx"), compressed.shape[2]):
        gram = summed_gram(compressed)
    else:
        gram = unpacked_gram(lax.psum(packed_gram(compressed), "gx"), compressed.shape[2])
    basis_two, turned = subspace(gram, start)
    core = jnp.einsum("krj,sj->krs", compressed, turned, precision=lax.Precision.HIGH)
    return (basis_two, core)


def solution(mesh):
    in_specs = (P("grp", "gx", None), P("grp", None), P())
    out_specs = (P("grp", None), P(("grp", "gx"), None, None))
    return jax.shard_map(body, mesh=mesh, in_specs=in_specs, out_specs=out_specs, check_vma=False)
```

```python
import jax
import jax.numpy as jnp
from jax import lax
from jax.experimental import pallas as pl
from jax.experimental.pallas import tpu as pltpu
from jax.sharding import PartitionSpec as P

ITERS = 4
BLOCK = 128
SUB = 8
HIGHEST = lax.Precision.HIGHEST


def packed_gram(compressed):
    width = compressed.shape[2]
    rows = [
        jnp.einsum("kri,krj->ij", compressed[:, :, at:at + BLOCK], compressed[:, :, at:], precision=HIGHEST)
        for at in range(0, width, BLOCK)
    ]
    return jnp.concatenate(rows, axis=1)


def unpacked_gram(packed, width):
    rows, offset = [], 0
    for at in range(0, width, BLOCK):
        rows.append(packed[:, offset:offset + width - at])
        offset += width - at
    whole = []
    for a in range(len(rows)):
        below = [rows[b][:, (a - b) * BLOCK:(a - b + 1) * BLOCK].T for b in range(a)]
        whole.append(jnp.concatenate(below + [rows[a]], axis=1))
    return jnp.concatenate(whole, axis=0)


def block_inverse(block):
    size = block.shape[0]
    sub = lax.broadcasted_iota(jnp.int32, (SUB, size), 0)
    lane = lax.broadcasted_iota(jnp.int32, (SUB, size), 1)
    tiles = size // SUB
    left = [block[t * SUB:(t + 1) * SUB, :] for t in range(tiles)]
    right = [jnp.where(lane == sub + t * SUB, 1.0, 0.0).astype(jnp.float32) for t in range(tiles)]
    pairs = range(0, SUB, 2)

    def row(tile, at):
        return jnp.broadcast_to(tile[at:at + 1, :], (SUB, size))

    def column(tile, at):
        return jnp.broadcast_to(tile[:, at:at + 1], (SUB, size))

    for tile in range(tiles):
        cols = [column(left[tile], tile * SUB + k) for k in range(SUB)]
        d = [[row(cols[l], k) for l in range(k + 1)] for k in range(SUB)]
        g = [[None] * SUB for k in range(SUB)]
        inverse = {}
        for a in pairs:
            b = a + 1
            inverse[a] = 1.0 / (d[a][a] * d[b][b] - d[b][a] * d[b][a])
            for i in range(b + 1, SUB):
                g[i][a] = (d[b][b] * d[i][a] - d[b][a] * d[i][b]) * inverse[a]
                g[i][b] = (d[a][a] * d[i][b] - d[b][a] * d[i][a]) * inverse[a]
            for i in range(b + 1, SUB):
                for l in range(b + 1, i + 1):
                    d[i][l] = d[i][l] - (g[i][a] * d[l][a] + g[i][b] * d[l][b])

        def forward(v):
            v = list(v)
            for a in pairs:
                for i in range(a + 2, SUB):
                    v[i] = v[i] - (g[i][a] * v[a] + g[i][a + 1] * v[a + 1])
            return v

        def backward(v):
            w = [None] * SUB
            for a in pairs:
                b = a + 1
                w[a] = (d[b][b] * v[a] - d[b][a] * v[b]) * inverse[a]
                w[b] = (d[a][a] * v[b] - d[b][a] * v[a]) * inverse[a]
            for a in reversed(pairs):
                for j in range(a):
                    w[j] = w[j] - (g[a][j] * w[a] + g[a + 1][j] * w[a + 1])
            return w

        wm = backward(forward([row(left[tile], k) for k in range(SUB)]))
        vn = forward([row(right[tile], k) for k in range(SUB)])
        wn = backward(vn)
        done = right[tile]
        for a in pairs:
            b = a + 1
            ratio = d[b][a] / d[a][a]
            done = jnp.where(sub == a, vn[a] * lax.rsqrt(d[a][a]), done)
            done = jnp.where(sub == b, (vn[b] - ratio * vn[a]) * lax.rsqrt(d[b][b] - ratio * d[b][a]), done)
        right[tile] = done
        for t in range(tile + 1, tiles):
            c = [column(left[t], tile * SUB + k) for k in range(SUB)]

            def total(w):
                p = [c[k] * w[k] for k in range(SUB)]
                return ((p[0] + p[1]) + (p[2] + p[3])) + ((p[4] + p[5]) + (p[6] + p[7]))

            left[t] = left[t] - total(wm)
            right[t] = right[t] - total(wn)
    return jnp.concatenate(right, axis=0)


def dot_t(a, b):
    return lax.dot_general(a, b, (((1,), (1,)), ((), ())), precision=HIGHEST, preferred_element_type=jnp.float32)


def dot(a, b):
    return jnp.dot(a, b, precision=HIGHEST, preferred_element_type=jnp.float32)


def halves_of(value):
    high = value.astype(jnp.bfloat16)
    return high, (value - high.astype(jnp.float32)).astype(jnp.bfloat16)


def dot_halves(a, b):
    def one(x, y):
        return jnp.dot(x, y, preferred_element_type=jnp.float32)

    return one(a[0], b[0]) + (one(a[1], b[0]) + one(a[0], b[1]))


def factor_inverse(cross, inverse_ref, work_ref, part_ref):
    size = cross.shape[0]
    half = size // 2
    eye = lax.broadcasted_iota(jnp.int32, (size, size), 0) == lax.broadcasted_iota(jnp.int32, (size, size), 1)
    diagonal = jnp.where(eye, cross, 0.0)
    along = lax.rsqrt(jnp.sum(diagonal, axis=0, keepdims=True))
    down = lax.rsqrt(jnp.sum(diagonal, axis=1, keepdims=True))
    work_ref[...] = cross * down * along
    part_ref[0] = work_ref[:half, :half]

    def step(index, carry):
        part_ref[index] = block_inverse(part_ref[index])

        @pl.when(index == 0)
        def _():
            side = dot_t(work_ref[half:, :half], part_ref[0])
            work_ref[half:, :half] = side
            part_ref[1] = work_ref[half:, half:] - dot_t(side, side)

        return carry

    lax.fori_loop(0, 2, step, 0)
    first, second = part_ref[0], part_ref[1]
    corner = -dot(dot(second, work_ref[half:, :half]), first)
    inverse_ref[:half, :half] = first * along[:, :half]
    inverse_ref[:half, half:] = jnp.zeros((half, half), jnp.float32)
    inverse_ref[half:, :half] = corner * along[:, :half]
    inverse_ref[half:, half:] = second * along[:, half:]


def subspace_kernel(gram_ref, start_ref, basis_ref, turned_ref, high_ref, low_ref, product_ref, inverse_ref, work_ref,
                    part_ref):
    high_ref[...], low_ref[...] = halves_of(gram_ref[...])
    turned_ref[...] = start_ref[...].T

    def step(index, carry):
        product_ref[...] = dot_halves(halves_of(turned_ref[...]), (high_ref[...], low_ref[...]))
        product = product_ref[...]
        factor_inverse(dot_t(product, product), inverse_ref, work_ref, part_ref)
        turned_ref[...] = dot_halves(halves_of(inverse_ref[...]), halves_of(product_ref[...]))
        return carry

    lax.fori_loop(0, ITERS, step, 0)
    basis_ref[...] = turned_ref[...].T


def subspace(gram, start):
    width, rank = start.shape
    vmem = pl.BlockSpec(memory_space=pltpu.VMEM)
    return pl.pallas_call(
        subspace_kernel,
        out_shape=(jax.ShapeDtypeStruct((width, rank), jnp.float32), jax.ShapeDtypeStruct((rank, width), jnp.float32)),
        in_specs=[vmem, vmem],
        out_specs=(vmem, vmem),
        scratch_shapes=[
            pltpu.VMEM((width, width), jnp.bfloat16),
            pltpu.VMEM((width, width), jnp.bfloat16),
            pltpu.VMEM((rank, width), jnp.float32),
            pltpu.VMEM((rank, rank), jnp.float32),
            pltpu.VMEM((rank, rank), jnp.float32),
            pltpu.VMEM((2, rank // 2, rank // 2), jnp.float32),
        ],
        compiler_params=pltpu.CompilerParams(vmem_limit_bytes=40 * 2**20),
        name="subspace",
    )(gram, start)


HALVES = ((0, 1, 5), (2, 3, 4, 6, 7))


def use_kernel(ranks, width):
    return ranks == 16 and width == 8 * BLOCK


def sum_kernel(plane_ref, gram_ref, part_ref, high_ref, low_ref, turned_high_ref, turned_low_ref, total, side, near, far, near_sum, far_sum, send_sems, recv_sems):
    me = lax.axis_index("gx")
    c, b, a = lax.rem(me, 2), lax.rem(me // 2, 2), me // 4
    sibling = me + 1 - 2 * c
    across = me + 2 - 4 * b
    others = [lax.rem(a + d, 4) * 4 + b * 2 + c for d in (1, 2, 3)]
    places = [lax.rem(a + d, 4) for d in (1, 2, 3)]

    barrier = pltpu.get_barrier_semaphore()
    for device in [sibling, across] + others:
        pl.semaphore_signal(barrier, inc=1, device_id={"gx": device}, device_id_type=pl.DeviceIdType.MESH)

    high_ref[...], low_ref[...] = halves_of(plane_ref[...])
    turned_high_ref[...], turned_low_ref[...] = halves_of(plane_ref[...].T)

    def multiply(h):
        offset = 0
        for r in HALVES[h]:
            at = r * BLOCK
            wide = plane_ref.shape[1] - at
            part_ref[h, :, offset:offset + wide] = dot_halves(
                (turned_high_ref[at:at + BLOCK, :], turned_low_ref[at:at + BLOCK, :]),
                (high_ref[:, at:], low_ref[:, at:]))
            offset += wide

    multiply(0)
    pl.semaphore_wait(barrier, 5)

    def send(slot, source, target, device):
        copy = pltpu.make_async_remote_copy(
            src_ref=source, dst_ref=target, send_sem=send_sems.at[slot], recv_sem=recv_sems.at[slot],
            device_id={"gx": device}, device_id_type=pl.DeviceIdType.MESH)
        copy.start()
        return copy

    def rows(start, count):
        return pl.ds(pl.multiple_of(start, SUB), count)

    def finish(copies):
        for copy in copies:
            copy.wait()

    scatter = [send(0, part_ref.at[0, rows((1 - c) * 64, 64)], side.at[0], sibling)]
    multiply(1)
    scatter.append(send(1, part_ref.at[1, rows((1 - c) * 64, 64)], side.at[1], sibling))
    scatter[0].wait()
    side[0] = side[0] + part_ref[0, rows(c * 64, 64), :]
    first_near = send(2, side.at[0, rows((1 - b) * 32, 32)], near.at[0, pl.ds(0, 32)], across)
    scatter[1].wait()
    side[1] = side[1] + part_ref[1, rows(c * 64, 64), :]
    first_far = [
        send(3 + d, side.at[1, rows(places[d] * 16, 16)], far.at[1, d, pl.ds(0, 16)], others[d]) for d in range(3)
    ]
    first_near.wait()
    near_sum[...] = side[0, rows(b * 32, 32), :] + near[0]
    second_far = [
        send(6 + d, near_sum.at[rows(places[d] * 8, 8)], far.at[0, d, pl.ds(0, 8)], others[d]) for d in range(3)
    ]
    finish(first_far)
    far_sum[...] = side[1, rows(a * 16, 16), :] + (far[1, 0] + far[1, 1] + far[1, 2])
    second_near = send(9, far_sum.at[rows((1 - b) * 8, 8)], near.at[1, pl.ds(0, 8)], across)
    finish(second_far)
    own_first = c * 64 + b * 32 + a * 8
    total[0, rows(own_first, 8), :] = near_sum[rows(a * 8, 8), :] + (
        far[0, 0, :8, :] + far[0, 1, :8, :] + far[0, 2, :8, :])
    piece = total.at[0, rows(own_first, 8)]
    gather_far = [send(10 + d, piece, piece, others[d]) for d in range(3)]
    second_near.wait()
    own_second = c * 64 + a * 16 + b * 8
    total[1, rows(own_second, 8), :] = far_sum[rows(b * 8, 8), :] + near[1, :8, :]
    piece = total.at[1, rows(own_second, 8)]
    gather_near = send(13, piece, piece, across)
    finish(gather_far)
    piece = total.at[0, rows(c * 64 + b * 32, 32)]
    last_near = send(14, piece, piece, across)
    gather_near.wait()
    piece = total.at[1, rows(c * 64 + a * 16, 16)]
    last_far = [send(15 + d, piece, piece, others[d]) for d in range(3)]
    last_near.wait()
    piece = total.at[0, rows(c * 64, 64)]
    gather = [send(18, piece, piece, sibling)]
    finish(last_far)
    piece = total.at[1, rows(c * 64, 64)]
    gather.append(send(19, piece, piece, sibling))
    for h in (0, 1):
        gather[h].wait()
        offset = 0
        for r in HALVES[h]:
            for s in range(r, 8):
                tile = total[h, :, offset * BLOCK:(offset + 1) * BLOCK]
                gram_ref[r * BLOCK:(r + 1) * BLOCK, s * BLOCK:(s + 1) * BLOCK] = tile
                if s != r:
                    gram_ref[s * BLOCK:(s + 1) * BLOCK, r * BLOCK:(r + 1) * BLOCK] = tile.T
                offset += 1


def summed_gram(compressed):
    width = compressed.shape[2]
    rank = compressed.shape[1]
    columns = sum(8 - r for r in HALVES[0]) * BLOCK
    vmem = pl.BlockSpec(memory_space=pltpu.VMEM)
    return pl.pallas_call(
        sum_kernel,
        out_shape=jax.ShapeDtypeStruct((width, width), jnp.float32),
        in_specs=[vmem],
        out_specs=vmem,
        scratch_shapes=[
            pltpu.VMEM((2, BLOCK, columns), jnp.float32),
            pltpu.VMEM((rank, width), jnp.bfloat16),
            pltpu.VMEM((rank, width), jnp.bfloat16),
            pltpu.VMEM((width, rank), jnp.bfloat16),
            pltpu.VMEM((width, rank), jnp.bfloat16),
            pltpu.VMEM((2, BLOCK, columns), jnp.float32),
            pltpu.VMEM((2, 64, columns), jnp.float32),
            pltpu.VMEM((2, 32, columns), jnp.float32),
            pltpu.VMEM((2, 3, 16, columns), jnp.float32),
            pltpu.VMEM((32, columns), jnp.float32),
            pltpu.VMEM((16, columns), jnp.float32),
            pltpu.SemaphoreType.DMA((20,)),
            pltpu.SemaphoreType.DMA((20,)),
        ],
        compiler_params=pltpu.CompilerParams(collective_id=0, has_side_effects=True, vmem_limit_bytes=40 * 2**20),
        name="sum_gram",
    )(compressed[0])


def compress_kernel(field_ref, basis_ref, out_ref, first, second, partial, arrived, high_ref, low_ref, send_sems,
                    recv_sems, local_sems):
    me = lax.axis_index("gx")
    half, place = me // 8, lax.rem(me, 8)
    partner = lax.rem(me + 8, 16)
    places = [lax.rem(place + d, 8) for d in range(1, 8)]
    depth = field_ref.shape[1]

    barrier = pltpu.get_barrier_semaphore()
    for device in [half * 8 + p for p in places] + [partner]:
        pl.semaphore_signal(barrier, inc=1, device_id={"gx": device}, device_id_type=pl.DeviceIdType.MESH)
    pl.semaphore_wait(barrier, 8)

    def send(slot, source, target, device):
        copy = pltpu.make_async_remote_copy(
            src_ref=source, dst_ref=target, send_sem=send_sems.at[slot], recv_sem=recv_sems.at[slot],
            device_id={"gx": device}, device_id_type=pl.DeviceIdType.MESH)
        copy.start()
        return copy

    def send_first(d):
        return send(d, field_ref.at[(1 - half) * 8 + places[d]], first.at[place], half * 8 + places[d])

    def send_second(d):
        return send(7 + d, field_ref.at[half * 8 + places[d]], second.at[place], half * 8 + places[d])

    firsts = [send_first(d) for d in range(7)]
    own = [
        pltpu.make_async_copy(field_ref.at[partner], first.at[place], local_sems.at[0]),
        pltpu.make_async_copy(field_ref.at[me], second.at[place], local_sems.at[1]),
    ]
    for copy in own:
        copy.start()
    rows = basis_ref[pl.ds(pl.multiple_of(half * (8 * depth), 8), 8 * depth), :]
    high_ref[...], low_ref[...] = halves_of(rows.T)

    def compress(source, target):
        width = target.shape[1]
        for at in range(0, width, 256):
            block = source[:, :, at:at + 256].reshape(8 * depth, 256)
            target[:, at:at + 256] = dot_halves((high_ref[...], low_ref[...]), halves_of(block))

    for copy in own:
        copy.wait()
    for copy in firsts[:4]:
        copy.wait()
    seconds = [send_second(d) for d in range(3)]
    for copy in firsts[4:]:
        copy.wait()
    compress(first, partial)
    crossing = send(14, partial, arrived, partner)
    seconds += [send_second(d) for d in range(3, 7)]
    for copy in seconds:
        copy.wait()
    compress(second, out_ref)
    crossing.wait()
    out_ref[...] = out_ref[...] + arrived[...]


def compressed_plane(field, basis_one):
    planes, depth, width = field.shape
    rank = basis_one.shape[1]
    vmem = pl.BlockSpec(memory_space=pltpu.VMEM)
    out = pl.pallas_call(
        compress_kernel,
        out_shape=jax.ShapeDtypeStruct((rank, width), jnp.float32),
        in_specs=[pl.BlockSpec(memory_space=pl.ANY), vmem],
        out_specs=vmem,
        scratch_shapes=[
            pltpu.VMEM((8, depth, width), jnp.float32),
            pltpu.VMEM((8, depth, width), jnp.float32),
            pltpu.VMEM((rank, width), jnp.float32),
            pltpu.VMEM((rank, width), jnp.float32),
            pltpu.VMEM((rank, 8 * depth), jnp.bfloat16),
            pltpu.VMEM((rank, 8 * depth), jnp.bfloat16),
            pltpu.SemaphoreType.DMA((15,)),
            pltpu.SemaphoreType.DMA((15,)),
            pltpu.SemaphoreType.DMA((2,)),
        ],
        compiler_params=pltpu.CompilerParams(collective_id=1, has_side_effects=True, vmem_limit_bytes=40 * 2**20),
        name="compress",
    )(field, basis_one)
    return out[None]


def body(field, basis_one, start):
    if use_kernel(lax.axis_size("gx"), field.shape[2]) and field.shape[0] == 16:
        compressed = compressed_plane(field, basis_one)
        gram = summed_gram(compressed)
    else:
        planes = lax.all_to_all(field, "gx", split_axis=0, concat_axis=1, tiled=True)
        compressed = jnp.einsum("ir,kij->krj", basis_one, planes, precision=lax.Precision.HIGH)
        gram = unpacked_gram(lax.psum(packed_gram(compressed), "gx"), compressed.shape[2])
    basis_two, turned = subspace(gram, start)
    core = jnp.einsum("krj,sj->krs", compressed, turned, precision=lax.Precision.HIGH)
    return (basis_two, core)


def solution(mesh):
    in_specs = (P("grp", "gx", None), P("grp", None), P())
    out_specs = (P("grp", None), P(("grp", "gx"), None, None))
    return jax.shard_map(body, mesh=mesh, in_specs=in_specs, out_specs=out_specs, check_vma=False)
```

```python
import jax
import jax.numpy as jnp
from jax import lax
from jax.experimental import pallas as pl
from jax.experimental.pallas import tpu as pltpu
from jax.sharding import PartitionSpec as P

ITERS = 4
BLOCK = 128
SUB = 8
LIMITS = (140.0, 45.0)
HIGHEST = lax.Precision.HIGHEST


def packed_gram(compressed):
    width = compressed.shape[2]
    rows = [
        jnp.einsum("kri,krj->ij", compressed[:, :, at:at + BLOCK], compressed[:, :, at:], precision=HIGHEST)
        for at in range(0, width, BLOCK)
    ]
    return jnp.concatenate(rows, axis=1)


def unpacked_gram(packed, width):
    rows, offset = [], 0
    for at in range(0, width, BLOCK):
        rows.append(packed[:, offset:offset + width - at])
        offset += width - at
    whole = []
    for a in range(len(rows)):
        below = [rows[b][:, (a - b) * BLOCK:(a - b + 1) * BLOCK].T for b in range(a)]
        whole.append(jnp.concatenate(below + [rows[a]], axis=1))
    return jnp.concatenate(whole, axis=0)


def block_inverse(block):
    size = block.shape[0]
    sub = lax.broadcasted_iota(jnp.int32, (SUB, size), 0)
    lane = lax.broadcasted_iota(jnp.int32, (SUB, size), 1)
    tiles = size // SUB
    left = [block[t * SUB:(t + 1) * SUB, :] for t in range(tiles)]
    right = [jnp.where(lane == sub + t * SUB, 1.0, 0.0).astype(jnp.float32) for t in range(tiles)]
    pairs = range(0, SUB, 2)

    def row(tile, at):
        return jnp.broadcast_to(tile[at:at + 1, :], (SUB, size))

    def column(tile, at):
        return jnp.broadcast_to(tile[:, at:at + 1], (SUB, size))

    for tile in range(tiles):
        cols = [column(left[tile], tile * SUB + k) for k in range(SUB)]
        d = [[row(cols[l], k) for l in range(k + 1)] for k in range(SUB)]
        g = [[None] * SUB for k in range(SUB)]
        inverse = {}
        for a in pairs:
            b = a + 1
            inverse[a] = 1.0 / (d[a][a] * d[b][b] - d[b][a] * d[b][a])
            for i in range(b + 1, SUB):
                g[i][a] = (d[b][b] * d[i][a] - d[b][a] * d[i][b]) * inverse[a]
                g[i][b] = (d[a][a] * d[i][b] - d[b][a] * d[i][a]) * inverse[a]
            for i in range(b + 1, SUB):
                for l in range(b + 1, i + 1):
                    d[i][l] = d[i][l] - (g[i][a] * d[l][a] + g[i][b] * d[l][b])

        def forward(v):
            v = list(v)
            for a in pairs:
                for i in range(a + 2, SUB):
                    v[i] = v[i] - (g[i][a] * v[a] + g[i][a + 1] * v[a + 1])
            return v

        def backward(v):
            w = [None] * SUB
            for a in pairs:
                b = a + 1
                w[a] = (d[b][b] * v[a] - d[b][a] * v[b]) * inverse[a]
                w[b] = (d[a][a] * v[b] - d[b][a] * v[a]) * inverse[a]
            for a in reversed(pairs):
                for j in range(a):
                    w[j] = w[j] - (g[a][j] * w[a] + g[a + 1][j] * w[a + 1])
            return w

        wm = backward(forward([row(left[tile], k) for k in range(SUB)]))
        vn = forward([row(right[tile], k) for k in range(SUB)])
        wn = backward(vn)
        done = right[tile]
        for a in pairs:
            b = a + 1
            ratio = d[b][a] / d[a][a]
            done = jnp.where(sub == a, vn[a] * lax.rsqrt(d[a][a]), done)
            done = jnp.where(sub == b, (vn[b] - ratio * vn[a]) * lax.rsqrt(d[b][b] - ratio * d[b][a]), done)
        right[tile] = done
        for t in range(tile + 1, tiles):
            c = [column(left[t], tile * SUB + k) for k in range(SUB)]

            def total(w):
                p = [c[k] * w[k] for k in range(SUB)]
                return ((p[0] + p[1]) + (p[2] + p[3])) + ((p[4] + p[5]) + (p[6] + p[7]))

            left[t] = left[t] - total(wm)
            right[t] = right[t] - total(wn)
    return jnp.concatenate(right, axis=0)


def dot_t(a, b):
    return lax.dot_general(a, b, (((1,), (1,)), ((), ())), precision=HIGHEST, preferred_element_type=jnp.float32)


def dot(a, b):
    return jnp.dot(a, b, precision=HIGHEST, preferred_element_type=jnp.float32)


def halves_of(value):
    high = value.astype(jnp.bfloat16)
    return high, (value - high.astype(jnp.float32)).astype(jnp.bfloat16)


def dot_halves(a, b):
    def one(x, y):
        return jnp.dot(x, y, preferred_element_type=jnp.float32)

    return one(a[0], b[0]) + (one(a[1], b[0]) + one(a[0], b[1]))


def factor_inverse(cross, inverse_ref, work_ref, part_ref):
    size = cross.shape[0]
    half = size // 2
    eye = lax.broadcasted_iota(jnp.int32, (size, size), 0) == lax.broadcasted_iota(jnp.int32, (size, size), 1)
    diagonal = jnp.where(eye, cross, 0.0)
    along = lax.rsqrt(jnp.sum(diagonal, axis=0, keepdims=True))
    down = lax.rsqrt(jnp.sum(diagonal, axis=1, keepdims=True))
    work_ref[...] = cross * down * along
    part_ref[0] = work_ref[:half, :half]

    def step(index, carry):
        part_ref[index] = block_inverse(part_ref[index])

        @pl.when(index == 0)
        def _():
            side = dot_t(work_ref[half:, :half], part_ref[0])
            work_ref[half:, :half] = side
            part_ref[1] = work_ref[half:, half:] - dot_t(side, side)

        return carry

    lax.fori_loop(0, 2, step, 0)
    first, second = part_ref[0], part_ref[1]
    corner = -dot(dot(second, work_ref[half:, :half]), first)
    inverse_ref[:half, :half] = first * along[:, :half]
    inverse_ref[:half, half:] = jnp.zeros((half, half), jnp.float32)
    inverse_ref[half:, :half] = corner * along[:, :half]
    inverse_ref[half:, half:] = second * along[:, half:]
    return jnp.where(eye[:half, :half], jnp.maximum(first, second) + 0.0 * (first + second), 0.0)


def subspace_kernel(gram_ref, start_ref, basis_ref, turned_ref, high_ref, low_ref, product_ref, inverse_ref, work_ref,
                    part_ref):
    high_ref[...], low_ref[...] = halves_of(gram_ref[...])
    turned_ref[...] = start_ref[...].T


    def step(index, carry):
        full, poor = carry
        product_ref[...] = dot_halves(halves_of(turned_ref[...]), (high_ref[...], low_ref[...]))
        product = product_ref[...]
        limit = jnp.where(index == ITERS - 1, LIMITS[1], LIMITS[0])

        def factored():
            roots = factor_inverse(dot_t(product, product), inverse_ref, work_ref, part_ref)
            turned_ref[...] = dot_halves(halves_of(inverse_ref[...]), halves_of(product_ref[...]))
            return jnp.max(jnp.where(roots < limit, 0.0, 1.0))

        def scaled():
            turned_ref[...] = product * lax.rsqrt(jnp.sum(product * product, axis=1, keepdims=True))
            return 0.0

        last_of_pair = lax.rem(ITERS - 1 - index, 2) == 0
        return full, jnp.maximum(poor, lax.cond(full | last_of_pair, factored, scaled))

    def attempt(carry):
        count, _ = carry
        turned_ref[...] = start_ref[...].T
        _, poor = lax.fori_loop(0, ITERS, step, (count > 0, jnp.float32(0.0)))
        return count + 1, poor

    lax.while_loop(lambda carry: (carry[0] == 0) | ((carry[0] == 1) & (carry[1] > 0.0)), attempt,
                   (jnp.int32(0), jnp.float32(0.0)))
    basis_ref[...] = turned_ref[...].T


def subspace(gram, start):
    width, rank = start.shape
    vmem = pl.BlockSpec(memory_space=pltpu.VMEM)
    return pl.pallas_call(
        subspace_kernel,
        out_shape=(jax.ShapeDtypeStruct((width, rank), jnp.float32), jax.ShapeDtypeStruct((rank, width), jnp.float32)),
        in_specs=[vmem, vmem],
        out_specs=(vmem, vmem),
        scratch_shapes=[
            pltpu.VMEM((width, width), jnp.bfloat16),
            pltpu.VMEM((width, width), jnp.bfloat16),
            pltpu.VMEM((rank, width), jnp.float32),
            pltpu.VMEM((rank, rank), jnp.float32),
            pltpu.VMEM((rank, rank), jnp.float32),
            pltpu.VMEM((2, rank // 2, rank // 2), jnp.float32),
        ],
        compiler_params=pltpu.CompilerParams(vmem_limit_bytes=40 * 2**20),
        name="subspace",
    )(gram, start)


HALVES = ((0, 1, 5), (2, 3, 4, 6, 7))


def use_kernel(ranks, width):
    return ranks == 16 and width == 8 * BLOCK


def sum_kernel(plane_ref, gram_ref, part_ref, high_ref, low_ref, turned_high_ref, turned_low_ref, total, side, near, far, near_sum, far_sum, send_sems, recv_sems):
    me = lax.axis_index("gx")
    c, b, a = lax.rem(me, 2), lax.rem(me // 2, 2), me // 4
    sibling = me + 1 - 2 * c
    across = me + 2 - 4 * b
    others = [lax.rem(a + d, 4) * 4 + b * 2 + c for d in (1, 2, 3)]
    places = [lax.rem(a + d, 4) for d in (1, 2, 3)]

    barrier = pltpu.get_barrier_semaphore()
    for device in [sibling, across] + others:
        pl.semaphore_signal(barrier, inc=1, device_id={"gx": device}, device_id_type=pl.DeviceIdType.MESH)

    high_ref[...], low_ref[...] = halves_of(plane_ref[...])
    turned_high_ref[...], turned_low_ref[...] = halves_of(plane_ref[...].T)

    def multiply(h):
        offset = 0
        for r in HALVES[h]:
            at = r * BLOCK
            wide = plane_ref.shape[1] - at
            part_ref[h, :, offset:offset + wide] = dot_halves(
                (turned_high_ref[at:at + BLOCK, :], turned_low_ref[at:at + BLOCK, :]),
                (high_ref[:, at:], low_ref[:, at:]))
            offset += wide

    multiply(0)
    pl.semaphore_wait(barrier, 5)

    def send(slot, source, target, device):
        copy = pltpu.make_async_remote_copy(
            src_ref=source, dst_ref=target, send_sem=send_sems.at[slot], recv_sem=recv_sems.at[slot],
            device_id={"gx": device}, device_id_type=pl.DeviceIdType.MESH)
        copy.start()
        return copy

    def rows(start, count):
        return pl.ds(pl.multiple_of(start, SUB), count)

    def finish(copies):
        for copy in copies:
            copy.wait()

    scatter = [send(0, part_ref.at[0, rows((1 - c) * 64, 64)], side.at[0], sibling)]
    multiply(1)
    scatter.append(send(1, part_ref.at[1, rows((1 - c) * 64, 64)], side.at[1], sibling))
    scatter[0].wait()
    side[0] = side[0] + part_ref[0, rows(c * 64, 64), :]
    first_near = send(2, side.at[0, rows((1 - b) * 32, 32)], near.at[0, pl.ds(0, 32)], across)
    scatter[1].wait()
    side[1] = side[1] + part_ref[1, rows(c * 64, 64), :]
    first_far = [
        send(3 + d, side.at[1, rows(places[d] * 16, 16)], far.at[1, d, pl.ds(0, 16)], others[d]) for d in range(3)
    ]
    first_near.wait()
    near_sum[...] = side[0, rows(b * 32, 32), :] + near[0]
    second_far = [
        send(6 + d, near_sum.at[rows(places[d] * 8, 8)], far.at[0, d, pl.ds(0, 8)], others[d]) for d in range(3)
    ]
    finish(first_far)
    far_sum[...] = side[1, rows(a * 16, 16), :] + (far[1, 0] + far[1, 1] + far[1, 2])
    second_near = send(9, far_sum.at[rows((1 - b) * 8, 8)], near.at[1, pl.ds(0, 8)], across)
    finish(second_far)
    own_first = c * 64 + b * 32 + a * 8
    total[0, rows(own_first, 8), :] = near_sum[rows(a * 8, 8), :] + (
        far[0, 0, :8, :] + far[0, 1, :8, :] + far[0, 2, :8, :])
    piece = total.at[0, rows(own_first, 8)]
    gather_far = [send(10 + d, piece, piece, others[d]) for d in range(3)]
    second_near.wait()
    own_second = c * 64 + a * 16 + b * 8
    total[1, rows(own_second, 8), :] = far_sum[rows(b * 8, 8), :] + near[1, :8, :]
    piece = total.at[1, rows(own_second, 8)]
    gather_near = send(13, piece, piece, across)
    finish(gather_far)
    piece = total.at[0, rows(c * 64 + b * 32, 32)]
    last_near = send(14, piece, piece, across)
    gather_near.wait()
    piece = total.at[1, rows(c * 64 + a * 16, 16)]
    last_far = [send(15 + d, piece, piece, others[d]) for d in range(3)]
    last_near.wait()
    piece = total.at[0, rows(c * 64, 64)]
    gather = [send(18, piece, piece, sibling)]
    finish(last_far)
    piece = total.at[1, rows(c * 64, 64)]
    gather.append(send(19, piece, piece, sibling))
    for h in (0, 1):
        gather[h].wait()
        offset = 0
        for r in HALVES[h]:
            for s in range(r, 8):
                tile = total[h, :, offset * BLOCK:(offset + 1) * BLOCK]
                gram_ref[r * BLOCK:(r + 1) * BLOCK, s * BLOCK:(s + 1) * BLOCK] = tile
                if s != r:
                    gram_ref[s * BLOCK:(s + 1) * BLOCK, r * BLOCK:(r + 1) * BLOCK] = tile.T
                offset += 1


def summed_gram(compressed):
    width = compressed.shape[2]
    rank = compressed.shape[1]
    columns = sum(8 - r for r in HALVES[0]) * BLOCK
    vmem = pl.BlockSpec(memory_space=pltpu.VMEM)
    return pl.pallas_call(
        sum_kernel,
        out_shape=jax.ShapeDtypeStruct((width, width), jnp.float32),
        in_specs=[vmem],
        out_specs=vmem,
        scratch_shapes=[
            pltpu.VMEM((2, BLOCK, columns), jnp.float32),
            pltpu.VMEM((rank, width), jnp.bfloat16),
            pltpu.VMEM((rank, width), jnp.bfloat16),
            pltpu.VMEM((width, rank), jnp.bfloat16),
            pltpu.VMEM((width, rank), jnp.bfloat16),
            pltpu.VMEM((2, BLOCK, columns), jnp.float32),
            pltpu.VMEM((2, 64, columns), jnp.float32),
            pltpu.VMEM((2, 32, columns), jnp.float32),
            pltpu.VMEM((2, 3, 16, columns), jnp.float32),
            pltpu.VMEM((32, columns), jnp.float32),
            pltpu.VMEM((16, columns), jnp.float32),
            pltpu.SemaphoreType.DMA((20,)),
            pltpu.SemaphoreType.DMA((20,)),
        ],
        compiler_params=pltpu.CompilerParams(collective_id=0, has_side_effects=True, vmem_limit_bytes=40 * 2**20),
        name="sum_gram",
    )(compressed[0])


def compress_kernel(field_ref, basis_ref, out_ref, first, second, partial, arrived, high_ref, low_ref, send_sems,
                    recv_sems, local_sems):
    me = lax.axis_index("gx")
    half, place = me // 8, lax.rem(me, 8)
    partner = lax.rem(me + 8, 16)
    places = [lax.rem(place + d, 8) for d in range(1, 8)]
    depth = field_ref.shape[1]

    barrier = pltpu.get_barrier_semaphore()
    for device in [half * 8 + p for p in places] + [partner]:
        pl.semaphore_signal(barrier, inc=1, device_id={"gx": device}, device_id_type=pl.DeviceIdType.MESH)
    pl.semaphore_wait(barrier, 8)

    def send(slot, source, target, device):
        copy = pltpu.make_async_remote_copy(
            src_ref=source, dst_ref=target, send_sem=send_sems.at[slot], recv_sem=recv_sems.at[slot],
            device_id={"gx": device}, device_id_type=pl.DeviceIdType.MESH)
        copy.start()
        return copy

    def send_first(d):
        return send(d, field_ref.at[(1 - half) * 8 + places[d]], first.at[place], half * 8 + places[d])

    def send_second(d):
        return send(7 + d, field_ref.at[half * 8 + places[d]], second.at[place], half * 8 + places[d])

    firsts = [send_first(d) for d in range(7)]
    own = [
        pltpu.make_async_copy(field_ref.at[partner], first.at[place], local_sems.at[0]),
        pltpu.make_async_copy(field_ref.at[me], second.at[place], local_sems.at[1]),
    ]
    for copy in own:
        copy.start()
    rows = basis_ref[pl.ds(pl.multiple_of(half * (8 * depth), 8), 8 * depth), :]
    high_ref[...], low_ref[...] = halves_of(rows.T)

    def compress(source, target):
        width = target.shape[1]
        for at in range(0, width, 256):
            block = source[:, :, at:at + 256].reshape(8 * depth, 256)
            target[:, at:at + 256] = dot_halves((high_ref[...], low_ref[...]), halves_of(block))

    for copy in own:
        copy.wait()
    for copy in firsts[:4]:
        copy.wait()
    seconds = [send_second(d) for d in range(3)]
    for copy in firsts[4:]:
        copy.wait()
    compress(first, partial)
    crossing = send(14, partial, arrived, partner)
    seconds += [send_second(d) for d in range(3, 7)]
    for copy in seconds:
        copy.wait()
    compress(second, out_ref)
    crossing.wait()
    out_ref[...] = out_ref[...] + arrived[...]


def compressed_plane(field, basis_one):
    planes, depth, width = field.shape
    rank = basis_one.shape[1]
    vmem = pl.BlockSpec(memory_space=pltpu.VMEM)
    out = pl.pallas_call(
        compress_kernel,
        out_shape=jax.ShapeDtypeStruct((rank, width), jnp.float32),
        in_specs=[pl.BlockSpec(memory_space=pl.ANY), vmem],
        out_specs=vmem,
        scratch_shapes=[
            pltpu.VMEM((8, depth, width), jnp.float32),
            pltpu.VMEM((8, depth, width), jnp.float32),
            pltpu.VMEM((rank, width), jnp.float32),
            pltpu.VMEM((rank, width), jnp.float32),
            pltpu.VMEM((rank, 8 * depth), jnp.bfloat16),
            pltpu.VMEM((rank, 8 * depth), jnp.bfloat16),
            pltpu.SemaphoreType.DMA((15,)),
            pltpu.SemaphoreType.DMA((15,)),
            pltpu.SemaphoreType.DMA((2,)),
        ],
        compiler_params=pltpu.CompilerParams(collective_id=1, has_side_effects=True, vmem_limit_bytes=40 * 2**20),
        name="compress",
    )(field, basis_one)
    return out[None]


def body(field, basis_one, start):
    if use_kernel(lax.axis_size("gx"), field.shape[2]) and field.shape[0] == 16:
        compressed = compressed_plane(field, basis_one)
        gram = summed_gram(compressed)
    else:
        planes = lax.all_to_all(field, "gx", split_axis=0, concat_axis=1, tiled=True)
        compressed = jnp.einsum("ir,kij->krj", basis_one, planes, precision=lax.Precision.HIGH)
        gram = unpacked_gram(lax.psum(packed_gram(compressed), "gx"), compressed.shape[2])
    basis_two, turned = subspace(gram, start)
    core = jnp.einsum("krj,sj->krs", compressed, turned, precision=lax.Precision.HIGH)
    return (basis_two, core)


def solution(mesh):
    in_specs = (P("grp", "gx", None), P("grp", None), P())
    out_specs = (P("grp", None), P(("grp", "gx"), None, None))
    return jax.shard_map(body, mesh=mesh, in_specs=in_specs, out_specs=out_specs, check_vma=False)
```

```python
import jax
import jax.numpy as jnp
from jax import lax
from jax.experimental import pallas as pl
from jax.experimental.pallas import tpu as pltpu
from jax.sharding import PartitionSpec as P

ITERS = 4
BLOCK = 128
SUB = 8
LIMITS = (140.0, 45.0)
HIGHEST = lax.Precision.HIGHEST


def packed_gram(compressed):
    width = compressed.shape[2]
    rows = [
        jnp.einsum("kri,krj->ij", compressed[:, :, at:at + BLOCK], compressed[:, :, at:], precision=HIGHEST)
        for at in range(0, width, BLOCK)
    ]
    return jnp.concatenate(rows, axis=1)


def unpacked_gram(packed, width):
    rows, offset = [], 0
    for at in range(0, width, BLOCK):
        rows.append(packed[:, offset:offset + width - at])
        offset += width - at
    whole = []
    for a in range(len(rows)):
        below = [rows[b][:, (a - b) * BLOCK:(a - b + 1) * BLOCK].T for b in range(a)]
        whole.append(jnp.concatenate(below + [rows[a]], axis=1))
    return jnp.concatenate(whole, axis=0)


def block_inverse(block):
    size = block.shape[0]
    sub = lax.broadcasted_iota(jnp.int32, (SUB, size), 0)
    lane = lax.broadcasted_iota(jnp.int32, (SUB, size), 1)
    tiles = size // SUB
    left = [block[t * SUB:(t + 1) * SUB, :] for t in range(tiles)]
    right = [jnp.where(lane == sub + t * SUB, 1.0, 0.0).astype(jnp.float32) for t in range(tiles)]
    pairs = range(0, SUB, 2)

    def row(tile, at):
        return jnp.broadcast_to(tile[at:at + 1, :], (SUB, size))

    def column(tile, at):
        return jnp.broadcast_to(tile[:, at:at + 1], (SUB, size))

    for tile in range(tiles):
        cols = [column(left[tile], tile * SUB + k) for k in range(SUB)]
        d = [[row(cols[l], k) for l in range(k + 1)] for k in range(SUB)]
        g = [[None] * SUB for k in range(SUB)]
        inverse = {}
        for a in pairs:
            b = a + 1
            inverse[a] = 1.0 / (d[a][a] * d[b][b] - d[b][a] * d[b][a])
            for i in range(b + 1, SUB):
                g[i][a] = (d[b][b] * d[i][a] - d[b][a] * d[i][b]) * inverse[a]
                g[i][b] = (d[a][a] * d[i][b] - d[b][a] * d[i][a]) * inverse[a]
            for i in range(b + 1, SUB):
                for l in range(b + 1, i + 1):
                    d[i][l] = d[i][l] - (g[i][a] * d[l][a] + g[i][b] * d[l][b])

        def forward(v):
            v = list(v)
            for a in pairs:
                for i in range(a + 2, SUB):
                    v[i] = v[i] - (g[i][a] * v[a] + g[i][a + 1] * v[a + 1])
            return v

        def backward(v):
            w = [None] * SUB
            for a in pairs:
                b = a + 1
                w[a] = (d[b][b] * v[a] - d[b][a] * v[b]) * inverse[a]
                w[b] = (d[a][a] * v[b] - d[b][a] * v[a]) * inverse[a]
            for a in reversed(pairs):
                for j in range(a):
                    w[j] = w[j] - (g[a][j] * w[a] + g[a + 1][j] * w[a + 1])
            return w

        wm = backward(forward([row(left[tile], k) for k in range(SUB)]))
        vn = forward([row(right[tile], k) for k in range(SUB)])
        wn = backward(vn)
        done = right[tile]
        for a in pairs:
            b = a + 1
            ratio = d[b][a] / d[a][a]
            done = jnp.where(sub == a, vn[a] * lax.rsqrt(d[a][a]), done)
            done = jnp.where(sub == b, (vn[b] - ratio * vn[a]) * lax.rsqrt(d[b][b] - ratio * d[b][a]), done)
        right[tile] = done
        for t in range(tile + 1, tiles):
            c = [column(left[t], tile * SUB + k) for k in range(SUB)]

            def total(w):
                p = [c[k] * w[k] for k in range(SUB)]
                return ((p[0] + p[1]) + (p[2] + p[3])) + ((p[4] + p[5]) + (p[6] + p[7]))

            left[t] = left[t] - total(wm)
            right[t] = right[t] - total(wn)
    return jnp.concatenate(right, axis=0)


def dot_t(a, b):
    return lax.dot_general(a, b, (((1,), (1,)), ((), ())), precision=HIGHEST, preferred_element_type=jnp.float32)


def dot(a, b):
    return jnp.dot(a, b, precision=HIGHEST, preferred_element_type=jnp.float32)


def halves_of(value):
    high = value.astype(jnp.bfloat16)
    return high, (value - high.astype(jnp.float32)).astype(jnp.bfloat16)


def dot_halves(a, b):
    def one(x, y):
        return jnp.dot(x, y, preferred_element_type=jnp.float32)

    return one(a[0], b[0]) + (one(a[1], b[0]) + one(a[0], b[1]))


def factor_inverse(cross, inverse_ref, work_ref, part_ref):
    size = cross.shape[0]
    half = size // 2
    eye = lax.broadcasted_iota(jnp.int32, (size, size), 0) == lax.broadcasted_iota(jnp.int32, (size, size), 1)
    diagonal = jnp.where(eye, cross, 0.0)
    along = lax.rsqrt(jnp.sum(diagonal, axis=0, keepdims=True))
    down = lax.rsqrt(jnp.sum(diagonal, axis=1, keepdims=True))
    work_ref[...] = cross * down * along
    part_ref[0] = work_ref[:half, :half]

    def step(index, carry):
        part_ref[index] = block_inverse(part_ref[index])

        @pl.when(index == 0)
        def _():
            side = dot_t(work_ref[half:, :half], part_ref[0])
            work_ref[half:, :half] = side
            part_ref[1] = work_ref[half:, half:] - dot_t(side, side)

        return carry

    lax.fori_loop(0, 2, step, 0)
    first, second = part_ref[0], part_ref[1]
    corner = -dot(dot(second, work_ref[half:, :half]), first)
    inverse_ref[:half, :half] = first * along[:, :half]
    inverse_ref[:half, half:] = jnp.zeros((half, half), jnp.float32)
    inverse_ref[half:, :half] = corner * along[:, :half]
    inverse_ref[half:, half:] = second * along[:, half:]
    return jnp.where(eye[:half, :half], jnp.maximum(first, second) + 0.0 * (first + second), 0.0)


def subspace_kernel(gram_ref, start_ref, basis_ref, turned_ref, product_ref, inverse_ref, work_ref, part_ref):
    turned_ref[...] = start_ref[...].T


    def step(index, carry):
        full, poor = carry
        product_ref[...] = dot(turned_ref[...], gram_ref[...])
        product = product_ref[...]
        limit = jnp.where(index == ITERS - 1, LIMITS[1], LIMITS[0])

        def factored():
            roots = factor_inverse(dot_t(product, product), inverse_ref, work_ref, part_ref)
            turned_ref[...] = dot_halves(halves_of(inverse_ref[...]), halves_of(product_ref[...]))
            return jnp.max(jnp.where(roots < limit, 0.0, 1.0))

        def scaled():
            turned_ref[...] = product * lax.rsqrt(jnp.sum(product * product, axis=1, keepdims=True))
            return 0.0

        last_of_pair = lax.rem(ITERS - 1 - index, 2) == 0
        return full, jnp.maximum(poor, lax.cond(full | last_of_pair, factored, scaled))

    def attempt(carry):
        count, _ = carry
        turned_ref[...] = start_ref[...].T
        _, poor = lax.fori_loop(0, ITERS, step, (count > 0, jnp.float32(0.0)))
        return count + 1, poor

    lax.while_loop(lambda carry: (carry[0] == 0) | ((carry[0] == 1) & (carry[1] > 0.0)), attempt,
                   (jnp.int32(0), jnp.float32(0.0)))
    basis_ref[...] = turned_ref[...].T


def subspace(gram, start):
    width, rank = start.shape
    vmem = pl.BlockSpec(memory_space=pltpu.VMEM)
    return pl.pallas_call(
        subspace_kernel,
        out_shape=(jax.ShapeDtypeStruct((width, rank), jnp.float32), jax.ShapeDtypeStruct((rank, width), jnp.float32)),
        in_specs=[vmem, vmem],
        out_specs=(vmem, vmem),
        scratch_shapes=[
            pltpu.VMEM((rank, width), jnp.float32),
            pltpu.VMEM((rank, rank), jnp.float32),
            pltpu.VMEM((rank, rank), jnp.float32),
            pltpu.VMEM((2, rank // 2, rank // 2), jnp.float32),
        ],
        compiler_params=pltpu.CompilerParams(vmem_limit_bytes=40 * 2**20),
        name="subspace",
    )(gram, start)


CHUNKS = ((0, 7), (1, 6), (2, 5), (3, 4))


def use_kernel(ranks, width):
    return ranks == 16 and width == 8 * BLOCK


def sum_kernel(plane_ref, gram_ref, part_ref, high_ref, low_ref, turned_high_ref, turned_low_ref, total, side, near,
               far, near_sum, send_sems, recv_sems):
    me = lax.axis_index("gx")
    c, b, a = lax.rem(me, 2), lax.rem(me // 2, 2), me // 4
    sibling = me + 1 - 2 * c
    across = me + 2 - 4 * b
    places = [lax.rem(a + d, 4) for d in (1, 2, 3)]
    others = [place * 4 + b * 2 + c for place in places]

    barrier = pltpu.get_barrier_semaphore()
    for device in [sibling, across] + others:
        pl.semaphore_signal(barrier, inc=1, device_id={"gx": device}, device_id_type=pl.DeviceIdType.MESH)

    high_ref[...], low_ref[...] = halves_of(plane_ref[...])
    turned_high_ref[...], turned_low_ref[...] = halves_of(plane_ref[...].T)

    def send(slot, source, target, device):
        copy = pltpu.make_async_remote_copy(
            src_ref=source, dst_ref=target, send_sem=send_sems.at[slot], recv_sem=recv_sems.at[slot],
            device_id={"gx": device}, device_id_type=pl.DeviceIdType.MESH)
        copy.start()
        return copy

    def rows(start, count):
        return pl.ds(pl.multiple_of(start, SUB), count)

    def spread(q, slot, start, count, devices):
        piece = total.at[q, rows(start, count)]
        flying[q] = [send(q * 10 + slot + d, piece, piece, devices[d]) for d in range(len(devices))]

    def arrive(q):
        for copy in flying[q]:
            copy.wait()

    def multiply(q):
        offset = 0
        for r in CHUNKS[q]:
            at = r * BLOCK
            wide = plane_ref.shape[1] - at
            part_ref[q, :, offset:offset + wide] = dot_halves(
                (turned_high_ref[at:at + BLOCK, :], turned_low_ref[at:at + BLOCK, :]),
                (high_ref[:, at:], low_ref[:, at:]))
            offset += wide

    def begin(q):
        multiply(q)
        if q == 0:
            pl.semaphore_wait(barrier, 5)
        flying[q] = [send(q * 10, part_ref.at[q, rows((1 - c) * 64, 64)], side.at[q], sibling)]

    def scatter_near(q):
        arrive(q)
        side[q] = side[q] + part_ref[q, rows(c * 64, 64), :]
        flying[q] = [send(q * 10 + 1, side.at[q, rows((1 - b) * 32, 32)], near.at[q], across)]

    def scatter_far(q):
        arrive(q)
        near_sum[q] = side[q, rows(b * 32, 32), :] + near[q]
        flying[q] = [
            send(q * 10 + 2 + d, near_sum.at[q, rows(places[d] * 8, 8)], far.at[q, d], others[d]) for d in range(3)
        ]

    def gather_far(q):
        arrive(q)
        start = c * 64 + b * 32 + a * 8
        total[q, rows(start, 8), :] = near_sum[q, rows(a * 8, 8), :] + (far[q, 0] + far[q, 1] + far[q, 2])
        spread(q, 5, start, 8, others)

    def gather_near(q):
        arrive(q)
        spread(q, 8, c * 64 + b * 32, 32, [across])

    def gather_side(q):
        arrive(q)
        spread(q, 9, c * 64, 64, [sibling])

    def unpack(q):
        arrive(q)
        offset = 0
        for r in CHUNKS[q]:
            for s in range(r, 8):
                tile = total[q, :, offset * BLOCK:(offset + 1) * BLOCK]
                gram_ref[r * BLOCK:(r + 1) * BLOCK, s * BLOCK:(s + 1) * BLOCK] = tile
                if s != r:
                    gram_ref[s * BLOCK:(s + 1) * BLOCK, r * BLOCK:(r + 1) * BLOCK] = tile.T
                offset += 1

    flying = {}
    stages = (begin, scatter_near, scatter_far, gather_far, gather_near, gather_side, unpack)
    for tick in range(len(CHUNKS) + len(stages) - 1):
        for at, stage in enumerate(stages):
            if 0 <= tick - at < len(CHUNKS):
                stage(tick - at)


def summed_gram(compressed):
    width = compressed.shape[2]
    rank = compressed.shape[1]
    columns = sum(8 - r for r in CHUNKS[0]) * BLOCK
    vmem = pl.BlockSpec(memory_space=pltpu.VMEM)
    return pl.pallas_call(
        sum_kernel,
        out_shape=jax.ShapeDtypeStruct((width, width), jnp.float32),
        in_specs=[vmem],
        out_specs=vmem,
        scratch_shapes=[
            pltpu.VMEM((4, BLOCK, columns), jnp.float32),
            pltpu.VMEM((rank, width), jnp.bfloat16),
            pltpu.VMEM((rank, width), jnp.bfloat16),
            pltpu.VMEM((width, rank), jnp.bfloat16),
            pltpu.VMEM((width, rank), jnp.bfloat16),
            pltpu.VMEM((4, BLOCK, columns), jnp.float32),
            pltpu.VMEM((4, 64, columns), jnp.float32),
            pltpu.VMEM((4, 32, columns), jnp.float32),
            pltpu.VMEM((4, 3, 8, columns), jnp.float32),
            pltpu.VMEM((4, 32, columns), jnp.float32),
            pltpu.SemaphoreType.DMA((40,)),
            pltpu.SemaphoreType.DMA((40,)),
        ],
        compiler_params=pltpu.CompilerParams(collective_id=0, has_side_effects=True, vmem_limit_bytes=40 * 2**20),
        name="sum_gram",
    )(compressed[0])


def compress_kernel(field_ref, basis_ref, out_ref, first, second, partial, arrived, high_ref, low_ref, send_sems,
                    recv_sems, local_sems):
    me = lax.axis_index("gx")
    half, place = me // 8, lax.rem(me, 8)
    partner = lax.rem(me + 8, 16)
    places = [lax.rem(place + d, 8) for d in range(1, 8)]
    depth = field_ref.shape[1]

    barrier = pltpu.get_barrier_semaphore()
    for device in [half * 8 + p for p in places] + [partner]:
        pl.semaphore_signal(barrier, inc=1, device_id={"gx": device}, device_id_type=pl.DeviceIdType.MESH)
    pl.semaphore_wait(barrier, 8)

    def send(slot, source, target, device):
        copy = pltpu.make_async_remote_copy(
            src_ref=source, dst_ref=target, send_sem=send_sems.at[slot], recv_sem=recv_sems.at[slot],
            device_id={"gx": device}, device_id_type=pl.DeviceIdType.MESH)
        copy.start()
        return copy

    def send_first(d):
        return send(d, field_ref.at[(1 - half) * 8 + places[d]], first.at[place], half * 8 + places[d])

    def send_second(d):
        return send(7 + d, field_ref.at[half * 8 + places[d]], second.at[place], half * 8 + places[d])

    firsts = [send_first(d) for d in range(7)]
    own = [
        pltpu.make_async_copy(field_ref.at[partner], first.at[place], local_sems.at[0]),
        pltpu.make_async_copy(field_ref.at[me], second.at[place], local_sems.at[1]),
    ]
    for copy in own:
        copy.start()
    rows = basis_ref[pl.ds(pl.multiple_of(half * (8 * depth), 8), 8 * depth), :]
    high_ref[...], low_ref[...] = halves_of(rows.T)

    def compress(source, target):
        width = target.shape[1]
        for at in range(0, width, 256):
            block = source[:, :, at:at + 256].reshape(8 * depth, 256)
            target[:, at:at + 256] = dot_halves((high_ref[...], low_ref[...]), halves_of(block))

    for copy in own:
        copy.wait()
    for copy in firsts[:4]:
        copy.wait()
    seconds = [send_second(d) for d in range(3)]
    for copy in firsts[4:]:
        copy.wait()
    compress(first, partial)
    crossing = send(14, partial, arrived, partner)
    seconds += [send_second(d) for d in range(3, 7)]
    for copy in seconds:
        copy.wait()
    compress(second, out_ref)
    crossing.wait()
    out_ref[...] = out_ref[...] + arrived[...]


def compressed_plane(field, basis_one):
    planes, depth, width = field.shape
    rank = basis_one.shape[1]
    vmem = pl.BlockSpec(memory_space=pltpu.VMEM)
    out = pl.pallas_call(
        compress_kernel,
        out_shape=jax.ShapeDtypeStruct((rank, width), jnp.float32),
        in_specs=[pl.BlockSpec(memory_space=pl.ANY), vmem],
        out_specs=vmem,
        scratch_shapes=[
            pltpu.VMEM((8, depth, width), jnp.float32),
            pltpu.VMEM((8, depth, width), jnp.float32),
            pltpu.VMEM((rank, width), jnp.float32),
            pltpu.VMEM((rank, width), jnp.float32),
            pltpu.VMEM((rank, 8 * depth), jnp.bfloat16),
            pltpu.VMEM((rank, 8 * depth), jnp.bfloat16),
            pltpu.SemaphoreType.DMA((15,)),
            pltpu.SemaphoreType.DMA((15,)),
            pltpu.SemaphoreType.DMA((2,)),
        ],
        compiler_params=pltpu.CompilerParams(collective_id=1, has_side_effects=True, vmem_limit_bytes=40 * 2**20),
        name="compress",
    )(field, basis_one)
    return out[None]


def body(field, basis_one, start):
    if use_kernel(lax.axis_size("gx"), field.shape[2]) and field.shape[0] == 16:
        compressed = compressed_plane(field, basis_one)
        gram = summed_gram(compressed)
    else:
        planes = lax.all_to_all(field, "gx", split_axis=0, concat_axis=1, tiled=True)
        compressed = jnp.einsum("ir,kij->krj", basis_one, planes, precision=lax.Precision.HIGH)
        gram = unpacked_gram(lax.psum(packed_gram(compressed), "gx"), compressed.shape[2])
    basis_two, turned = subspace(gram, start)
    core = jnp.einsum("krj,sj->krs", compressed, turned, precision=lax.Precision.HIGH)
    return (basis_two, core)


def solution(mesh):
    in_specs = (P("grp", "gx", None), P("grp", None), P())
    out_specs = (P("grp", None), P(("grp", "gx"), None, None))
    return jax.shard_map(body, mesh=mesh, in_specs=in_specs, out_specs=out_specs, check_vma=False)
```
